256 devices in a mesh: row: 8 (over z), col: 32 (over y, x, core).
Axes of the slice: x: 4, y: 4, z: 8, core: 2. Of those that a mesh axis runs over, the one named last changes fastest.
Arguments:
- tokens: bfloat16 [2560, 5120], P('col', 'row'), may hold values from -6 to 6
- cotangent: bfloat16 [2560, 5120], P('col', 'row'), may hold values from -1.5 to 1.5
- gate_weight: bfloat16 [5120, 8192], P('row', 'col'), may hold values from -0.078125 to 0.078125
- up_weight: bfloat16 [5120, 8192], P('row', 'col'), may hold values from -0.078125 to 0.078125
- down_weight: bfloat16 [8192, 5120], P('col', 'row'), may hold values from -0.0625 to 0.0625
Outputs:
- grad_tokens: float32 [2560, 5120], P('col', 'row')
- grad_gate_weight: float32 [5120, 8192], P('row', 'col')
- grad_up_weight: float32 [5120, 8192], P('row', 'col')
- grad_down_weight: float32 [8192, 5120], P('col', 'row')
The draws below stay inside these ranges and needn't reach their ends.
All inputs are finite; a program needn't handle non-finite values.
Results may differ from the reference program's by a relative error of at most 0.0029.
Values may be sent and summed in bfloat16 or wider, within the bound.
A program may use at most 64 MiB of HBM per device.

```python
import jax
import jax.numpy as jnp
from jax import lax

D = 5120
FF = 8192
TOKENS = 2560


def block_levels(key, extent, split, low, top_value):
    level = 1.0
    for dim, parts in split:
        heights = jax.random.uniform(jax.random.fold_in(jax.random.fold_in(key, 6), dim), (parts,), jnp.float32, low / len(split), top_value / len(split))
        level = level * jnp.repeat(jnp.exp(heights), extent[dim] // parts).reshape((-1,) + (1,) * (len(extent) - 1 - dim))
    return level


def gaussian(rng, extent, spread, reach, pieces=(), dtype=jnp.bfloat16):
    gain = block_levels(rng, extent, pieces, -0.22, 0.18) if pieces else 1.0
    entries = jax.random.normal(rng, extent, jnp.float32) * spread * gain
    return jnp.minimum(jnp.maximum(entries, -reach), reach).astype(dtype)


def setup_inputs(seed: int = 0) -> dict:
    key_list = jax.random.split(jax.random.key(seed), 6)
    tokens = gaussian(key_list[0], (TOKENS, D), 1.0, 6.0, ((0, 32), (1, 8)))
    cotangent = gaussian(key_list[1], (TOKENS, D), 0.25, 1.5, ((0, 32), (1, 8)))
    gate_weight = gaussian(key_list[2], (D, FF), D ** -0.5, 0.078125, ((0, 8), (1, 32)))
    up_weight = gaussian(key_list[3], (D, FF), D ** -0.5, 0.078125, ((0, 8), (1, 32)))
    down_weight = gaussian(key_list[4], (FF, D), FF ** -0.5, 0.0625, ((0, 32), (1, 8)))
    return dict(tokens=tokens, cotangent=cotangent, gate_weight=gate_weight, up_weight=up_weight, down_weight=down_weight)


def reference(tokens, cotangent, gate_weight, up_weight, down_weight):
    gate_proj = jnp.dot(tokens, gate_weight, preferred_element_type=jnp.float32)
    up_proj = jnp.dot(tokens, up_weight, preferred_element_type=jnp.float32)
    grad_hidden = lax.dot_general(cotangent, down_weight, (((1,), (1,)), ((), ())), preferred_element_type=jnp.float32)
    sigmoid_gate = jax.nn.sigmoid(gate_proj)
    silu_gate = gate_proj * sigmoid_gate
    hidden = (silu_gate * up_proj).astype(jnp.bfloat16)
    grad_up = (grad_hidden * silu_gate).astype(jnp.bfloat16)
    grad_gate = (grad_hidden * up_proj * sigmoid_gate * (1.0 + gate_proj * (1.0 - sigmoid_gate))).astype(jnp.bfloat16)
    contract_rows = (((0,), (0,)), ((), ()))
    grad_down_weight = lax.dot_general(hidden, cotangent, contract_rows, preferred_element_type=jnp.float32)
    grad_gate_weight = lax.dot_general(tokens, grad_gate, contract_rows, preferred_element_type=jnp.float32)
    grad_up_weight = lax.dot_general(tokens, grad_up, contract_rows, preferred_element_type=jnp.float32)
    contract_cols = (((1,), (1,)), ((), ()))
    grad_tokens = lax.dot_general(grad_gate, gate_weight, contract_cols, preferred_element_type=jnp.float32)
    grad_tokens = grad_tokens + lax.dot_general(grad_up, up_weight, contract_cols, preferred_element_type=jnp.float32)
    return grad_tokens, grad_gate_weight, grad_up_weight, grad_down_weight
```

```python
import jax
import jax.numpy as jnp
from jax import lax
from jax.experimental import pallas as pl
from jax.experimental.pallas import tpu as pltpu
from jax.sharding import PartitionSpec as P

MESH = pl.DeviceIdType.MESH
BF = jnp.bfloat16
F32 = jnp.float32

SLABS = 5
RS = 16
W = 640
H = 256
CH = 64
HALF = 32

A_A, A_B, A_D = 0, 3, 6
R_R, R_L = 10, 14
G_R, G_L = 18, 22
S_D, S_B, S_A = 26, 27, 30
NSEM = 33


def enc4(v):
    t = v * jnp.abs(v) * (2.0**40)
    return (t * jnp.abs(t)).astype(BF)


def dec4(w):
    w = w.astype(F32)
    a = jnp.maximum(jnp.abs(w), 1e-37)
    r = lax.rsqrt(a)
    return (w * r) * (lax.rsqrt(a * r) * (2.0**-20))


def enc2(v):
    return (v * jnp.abs(v)).astype(BF)


def dec2(w):
    w = w.astype(F32)
    return w * lax.rsqrt(jnp.maximum(jnp.abs(w), 1e-37))


def kernel(
    tok_hbm, cot_hbm, wg_hbm, wu_hbm, wd_hbm,
    gtok_hbm, gwg_hbm, gwu_hbm, gwd_hbm,
    own, xy, wgu, wd, part, rsend, rrecv, hid, gx, dsend, drecv, bsend, brecv, asend, arecv,
    gtok, gwgu, gwd,
    ssem, rsem, lsem,
):
    r = lax.axis_index("row")
    c = lax.axis_index("col")
    core = lax.rem(c, 2)
    x = lax.rem(lax.div(c, 2), 4)
    y = lax.div(c, 8)
    a = x + core * (y - x)
    b = y + core * (x - y)

    def col(a_, b_):
        x_ = a_ + core * (b_ - a_)
        y_ = b_ + core * (a_ - b_)
        return y_ * 8 + x_ * 2 + core

    def m4(v):
        return lax.rem(v + 8, 4)

    def m8(v):
        return lax.rem(v + 16, 8)

    right = (m8(r + 1), c)
    left = (m8(r - 1), c)
    peer = (r, c + 1 - 2 * core)
    adev = {d: (r, col(m4(a + d), b)) for d in (1, 2, 3)}
    bdev = {d: (r, col(a, m4(b + d))) for d in (1, 2, 3)}

    loads = [
        pltpu.make_async_copy(tok_hbm, own.at[0], lsem.at[0]),
        pltpu.make_async_copy(cot_hbm, own.at[1], lsem.at[1]),
        pltpu.make_async_copy(wg_hbm, wgu.at[:, pl.ds(0, H)], lsem.at[2]),
        pltpu.make_async_copy(wu_hbm, wgu.at[:, pl.ds(H, H)], lsem.at[3]),
        pltpu.make_async_copy(wd_hbm, wd, lsem.at[4]),
    ]
    for cp in loads:
        cp.start()

    barrier = pltpu.get_barrier_semaphore()
    partners = [right, left, peer] + [adev[d] for d in (1, 2, 3)] + [bdev[d] for d in (1, 2, 3)]
    for dev in partners:
        pl.semaphore_signal(barrier, inc=1, device_id=dev, device_id_type=MESH)
    pl.semaphore_wait(barrier, len(partners))

    sent = []

    def copy(src, dst, s, k, dev):
        return pltpu.make_async_remote_copy(
            src_ref=src, dst_ref=dst, send_sem=ssem.at[s, k], recv_sem=rsem.at[s, k],
            device_id=dev, device_id_type=MESH,
        )

    def send(src, dst, s, k, dev):
        cp = copy(src, dst, s, k, dev)
        cp.start()
        sent.append(cp)

    def recv(dst, s, k):
        copy(dst, dst, s, k, right).wait_recv()

    def pos(s, co, b_, a_):
        return xy.at[s, pl.ds(co * 16 + b_ * 4 + a_, 1)]

    def line(s, co, b_):
        return xy.at[s, pl.ds(co * 16 + b_ * 4, 4)]

    def chunk(ref, s, j, lo=0, n=CH):
        return ref.at[s, pl.ds(pl.multiple_of(j * CH + lo, 32), n)]

    def gather0(s):
        me = pos(s, core, b, a)
        for d in (1, 2, 3):
            send(me, me, s, A_A + d - 1, adev[d])

    def gather1(s):
        for d in (1, 2, 3):
            recv(pos(s, core, b, m4(a - d)), s, A_A + d - 1)
        row = line(s, core, b)
        for d in (1, 2, 3):
            send(row, row, s, A_B + d - 1, bdev[d])
        send(row, row, s, A_D, peer)

    def gather2(s):
        for d in (1, 3, 2):
            row = line(s, core, m4(b - d))
            recv(row, s, A_B + d - 1)
            send(row, row, s, A_D + d, peer)

    def project(s):
        for d in range(4):
            recv(line(s, 1 - core, m4(a - d)), s, A_D + d)
        xs = xy[s, :, 0].reshape(32 * RS, W)
        ys = xy[s, :, 1].reshape(32 * RS, W)
        part[s, :, 0 : 2 * H] = jnp.dot(xs, wgu[...], preferred_element_type=F32)
        part[s, :, 2 * H : 3 * H] = lax.dot_general(
            ys, wd[...], (((1,), (1,)), ((), ())), preferred_element_type=F32
        )

    def reduce_step(s, h):
        if h == 0:
            far = m8(r + 4)
            rsend[s, 0, 0, 0:HALF] = enc4(chunk(part, s, far, 0, HALF)[...])
            rsend[s, 1, 0, 0:HALF] = enc4(chunk(part, s, far, HALF, HALF)[...])
            for way, dev, k in ((0, right, R_R), (1, left, R_L)):
                send(
                    rsend.at[s, way, 0, pl.ds(0, HALF)],
                    rrecv.at[s, way, 0, pl.ds(0, HALF)],
                    s, k, dev,
                )
            return
        for way, dev, k, j in ((0, right, R_R, m8(r + 4 - h)), (1, left, R_L, m8(r - 4 + h))):
            if h == 1:
                got = rrecv.at[s, way, 0, pl.ds(0, HALF)]
                recv(got, s, k)
                near, rest = (0, HALF) if way == 0 else (HALF, 0)
                rsend[s, way, 1, near : near + HALF] = enc4(
                    chunk(part, s, j, near, HALF)[...] + dec4(got[...])
                )
                rsend[s, way, 1, rest : rest + HALF] = enc4(chunk(part, s, j, rest, HALF)[...])
            else:
                got = rrecv.at[s, way, h - 1]
                recv(got, s, k + h - 1)
                rsend[s, way, h] = enc4(chunk(part, s, j)[...] + dec4(got[...]))
            send(rsend.at[s, way, h], rrecv.at[s, way, h], s, k + h, dev)

    def activate(s):
        recv(rrecv.at[s, 0, 3], s, R_R + 3)
        recv(rrecv.at[s, 1, 3], s, R_L + 3)
        mine = chunk(part, s, r)
        total = mine[...] + dec4(rrecv[s, 0, 3]) + dec4(rrecv[s, 1, 3])
        g, u, gh = total[:, 0:H], total[:, H : 2 * H], total[:, 2 * H :]
        sg = jax.nn.sigmoid(g)
        silu = g * sg
        out = chunk(hid, s, r)
        out[:, 0:H] = (gh * u * sg * (1.0 + g * (1.0 - sg))).astype(BF)
        out[:, H : 2 * H] = (gh * silu).astype(BF)
        out[:, 2 * H :] = (silu * u).astype(BF)

    def spread_step(s, h):
        if h == 0:
            mine = chunk(hid, s, r)
            send(mine, mine, s, G_R, right)
            send(mine, mine, s, G_L, left)
            return
        if h <= 3:
            lo, hi = chunk(hid, s, m8(r - h)), chunk(hid, s, m8(r + h))
            recv(lo, s, G_R + h - 1)
            if h == 3:
                half = chunk(hid, s, m8(r - 3), 0, HALF)
                send(half, half, s, G_R + 3, right)
            else:
                send(lo, lo, s, G_R + h, right)
            recv(hi, s, G_L + h - 1)
            if h == 3:
                half = chunk(hid, s, m8(r + 3), HALF, HALF)
                send(half, half, s, G_L + 3, left)
            else:
                send(hi, hi, s, G_L + h, left)
            return
        recv(chunk(hid, s, m8(r + 4), 0, HALF), s, G_R + 3)
        recv(chunk(hid, s, m8(r + 4), HALF, HALF), s, G_L + 3)

    def token_grad(s):
        gx[...] = lax.dot_general(
            hid[s, :, 0 : 2 * H], wgu[...], (((1,), (1,)), ((), ())), preferred_element_type=F32
        )
        theirs = pl.ds(pl.multiple_of((1 - core) * 256, 256), 256)
        dsend[s] = enc2(gx[theirs])
        send(dsend.at[s], drecv.at[s], s, S_D, peer)

    def weight_grads(s):
        xs = xy[s, :, 0].reshape(32 * RS, W)
        ys = xy[s, :, 1].reshape(32 * RS, W)
        over = (((0,), (0,)), ((), ()))
        dgu = lax.dot_general(xs, hid[s, :, 0 : 2 * H], over, preferred_element_type=F32)
        dd = lax.dot_general(hid[s, :, 2 * H :], ys, over, preferred_element_type=F32)
        if s == 0:
            gwgu[...] = dgu
            gwd[...] = dd
        else:
            gwgu[...] += dgu
            gwd[...] += dd

    def scatter1(s):
        recv(drecv.at[s], s, S_D)
        gx[0:256] = gx[pl.ds(pl.multiple_of(core * 256, 256), 256)] + dec2(drecv[s])
        for d in (1, 2, 3):
            rows = pl.ds(pl.multiple_of(m4(b + d) * CH, CH), CH)
            bsend[s, d - 1] = enc2(gx[rows])
            send(bsend.at[s, d - 1], brecv.at[s, d - 1], s, S_B + d - 1, bdev[d])

    def scatter2(s):
        total = gx[pl.ds(pl.multiple_of(b * CH, CH), CH)]
        for d in (1, 2, 3):
            recv(brecv.at[s, d - 1], s, S_B + d - 1)
            total = total + dec2(brecv[s, d - 1])
        gx[0:CH] = total
        for d in (1, 2, 3):
            rows = pl.ds(pl.multiple_of(m4(a + d) * RS, RS), RS)
            asend[s, d - 1] = enc2(gx[rows])
            send(asend.at[s, d - 1], arecv.at[s, d - 1], s, S_A + d - 1, adev[d])
        gtok[s * RS : (s + 1) * RS] = gx[pl.ds(pl.multiple_of(a * RS, RS), RS)]

    def scatter3(s):
        total = gtok[s * RS : (s + 1) * RS]
        for d in (1, 2, 3):
            recv(arecv.at[s, d - 1], s, S_A + d - 1)
            total = total + dec2(arecv[s, d - 1])
        gtok[s * RS : (s + 1) * RS] = total

    def place_own():
        loads[0].wait()
        loads[1].wait()
        for s in range(SLABS):
            for k in range(2):
                xy[s, pl.ds(core * 16 + b * 4 + a, 1), k] = own[k, s * RS : (s + 1) * RS][None]

    def wait_weights():
        for cp in loads[2:]:
            cp.wait()

    tasks = [(-20.0, place_own), (-0.6, wait_weights)]
    for s in range(SLABS):
        t = 2.0 * s
        tasks.append((t - 12 if s < 2 else t - 3.5, lambda s=s: gather0(s)))
        tasks.append((t - 2.4, lambda s=s: gather1(s)))
        tasks.append((t - 1.4, lambda s=s: gather2(s)))
        tasks.append((t - 0.4, lambda s=s: project(s)))
        for h in range(4):
            tasks.append((t + h, lambda s=s, h=h: reduce_step(s, h)))
        tasks.append((t + 4, lambda s=s: activate(s)))
        for h in range(5):
            tasks.append((t + 4.1 + h, lambda s=s, h=h: spread_step(s, h)))
        tasks.append((t + 8.2, lambda s=s: token_grad(s)))
        tasks.append((t + 8.3, lambda s=s: weight_grads(s)))
        tasks.append((t + 8.7, lambda s=s: scatter1(s)))
        tasks.append((t + 9.7, lambda s=s: scatter2(s)))
        tasks.append((t + 11.3, lambda s=s: scatter3(s)))
    for _, task in sorted(tasks, key=lambda p: p[0]):
        task()

    stores = [
        pltpu.make_async_copy(gtok, gtok_hbm, lsem.at[0]),
        pltpu.make_async_copy(gwgu.at[:, pl.ds(0, H)], gwg_hbm, lsem.at[1]),
        pltpu.make_async_copy(gwgu.at[:, pl.ds(H, H)], gwu_hbm, lsem.at[2]),
        pltpu.make_async_copy(gwd, gwd_hbm, lsem.at[3]),
    ]
    for cp in stores:
        cp.start()
    for cp in sent:
        cp.wait_send()
    for cp in stores:
        cp.wait()


def per_device(tokens, cotangent, gate_weight, up_weight, down_weight):
    hbm = pl.BlockSpec(memory_space=pl.ANY)
    rows = 32 * RS
    vm = pltpu.VMEM
    return pl.pallas_call(
        kernel,
        out_shape=(
            jax.ShapeDtypeStruct((SLABS * RS, W), F32),
            jax.ShapeDtypeStruct((W, H), F32),
            jax.ShapeDtypeStruct((W, H), F32),
            jax.ShapeDtypeStruct((H, W), F32),
        ),
        in_specs=[hbm] * 5,
        out_specs=[hbm] * 4,
        scratch_shapes=[
            vm((2, SLABS * RS, W), BF),
            vm((SLABS, 32, 2, RS, W), BF),
            vm((W, 2 * H), BF),
            vm((H, W), BF),
            vm((SLABS, rows, 3 * H), F32),
            vm((SLABS, 2, 4, CH, 3 * H), BF),
            vm((SLABS, 2, 4, CH, 3 * H), BF),
            vm((SLABS, rows, 3 * H), BF),
            vm((rows, W), F32),
            vm((SLABS, 256, W), BF),
            vm((SLABS, 256, W), BF),
            vm((SLABS, 3, CH, W), BF),
            vm((SLABS, 3, CH, W), BF),
            vm((SLABS, 3, RS, W), BF),
            vm((SLABS, 3, RS, W), BF),
            vm((SLABS * RS, W), F32),
            vm((W, 2 * H), F32),
            vm((H, W), F32),
            pltpu.SemaphoreType.DMA((SLABS, NSEM)),
            pltpu.SemaphoreType.DMA((SLABS, NSEM)),
            pltpu.SemaphoreType.DMA((5,)),
        ],
        compiler_params=pltpu.CompilerParams(
            collective_id=0, has_side_effects=True, vmem_limit_bytes=58 * 2**20
        ),
        name="swiglu_backward",
    )(tokens, cotangent, gate_weight, up_weight, down_weight)


def solution(mesh):
    in_specs = (P("col", "row"), P("col", "row"), P("row", "col"), P("row", "col"), P("col", "row"))
    out_specs = (P("col", "row"), P("row", "col"), P("row", "col"), P("col", "row"))
    return jax.shard_map(
        per_device, mesh=mesh, in_specs=in_specs, out_specs=out_specs, check_vma=False
    )
```

```python
import jax
import jax.numpy as jnp
from jax import lax
from jax.experimental import pallas as pl
from jax.experimental.pallas import tpu as pltpu
from jax.sharding import PartitionSpec as P

MESH = pl.DeviceIdType.MESH
BF = jnp.bfloat16
F32 = jnp.float32

SLABS = 5
RS = 16
W = 640
H = 256
CH = 64
HALF = 32

FH = 128
ZW = 3 * FH

A_A, A_B, A_D = 0, 3, 6
S_D, S_B, S_A = 10, 14, 17
R_R, R_L = 20, 28
G_R, G_L = 36, 44
NSEM = 52


def enc4(v):
    t = v * jnp.abs(v) * (2.0**40)
    return (t * jnp.abs(t)).astype(BF)


def dec4(w):
    w = w.astype(F32)
    a = jnp.maximum(jnp.abs(w), 1e-37)
    r = lax.rsqrt(a)
    return (w * r) * (lax.rsqrt(a * r) * (2.0**-20))


def enc2(v):
    return (v * jnp.abs(v)).astype(BF)


def dec2(w):
    w = w.astype(F32)
    return w * lax.rsqrt(jnp.maximum(jnp.abs(w), 1e-37))


ORDER = (
    ("g0", 0), ("g0", 1), ("g1", 0), ("g1", 1), ("g2", 0), ("g0", 2), ("g0", 3), ("pj", 0, 0),
    ("r0", 0, 0), ("pj", 0, 1), ("r0", 0, 1), ("g2", 1), ("g0", 4), ("r1", 0, 0), ("g1", 2),
    ("r1", 0, 1), ("pj", 1, 0), ("r0", 1, 0), ("pj", 1, 1), ("r0", 1, 1), ("r2", 0, 0),
    ("r2", 0, 1), ("r1", 1, 0), ("g1", 3), ("g1", 4), ("r1", 1, 1), ("r3", 0, 0), ("g2", 2),
    ("r3", 0, 1), ("r2", 1, 0), ("r2", 1, 1), ("h0", 0, 0), ("h0", 0, 1), ("r3", 1, 0),
    ("pj", 2, 0), ("r3", 1, 1), ("r0", 2, 0), ("g2", 3), ("pj", 2, 1), ("h1", 0, 0),
    ("h1", 0, 1), ("h0", 1, 1), ("h0", 1, 0), ("pj", 3, 0), ("pj", 3, 1), ("h2", 0, 0),
    ("r0", 2, 1), ("r0", 3, 1), ("g2", 4), ("r0", 3, 0), ("r1", 2, 0), ("h1", 1, 1),
    ("r1", 3, 1), ("h1", 1, 0), ("r1", 2, 1), ("h2", 0, 1), ("r1", 3, 0), ("h2", 1, 0),
    ("r2", 2, 0), ("r2", 2, 1), ("pj", 4, 0), ("h2", 1, 1), ("tA", 1), ("pj", 4, 1), ("tA", 0),
    ("h3", 0, 0), ("uA", 0), ("r0", 4, 1), ("h3", 0, 1), ("r3", 2, 0), ("h3", 1, 1),
    ("h4", 0, 0), ("r2", 3, 0), ("r3", 2, 1), ("r1", 4, 1), ("h3", 1, 0), ("h0", 2, 0),
    ("h4", 1, 1), ("uA", 1), ("tB", 0), ("r2", 3, 1), ("r0", 4, 0), ("h4", 0, 1), ("r3", 3, 0),
    ("h0", 2, 1), ("uB", 0), ("tC", 0), ("r2", 4, 1), ("uC", 0), ("r1", 4, 0), ("h1", 2, 0),
    ("h1", 2, 1), ("r3", 3, 1), ("tB", 1), ("wg", 0), ("r3", 4, 1), ("s2", 0), ("h2", 2, 0),
    ("h2", 2, 1), ("h4", 1, 0), ("uB", 1), ("h0", 3, 0), ("tC", 1), ("r2", 4, 0), ("uC", 1),
    ("h0", 3, 1), ("h3", 2, 0), ("h3", 2, 1), ("wg", 1), ("h1", 3, 0), ("tA", 2), ("r3", 4, 0),
    ("tB", 2), ("h4", 2, 0), ("h0", 4, 1), ("h1", 3, 1), ("uA", 2), ("uB", 2), ("h2", 3, 0),
    ("h4", 2, 1), ("tC", 2), ("s2", 1), ("h0", 4, 0), ("h2", 3, 1), ("h1", 4, 1), ("uC", 2),
    ("tA", 3), ("h1", 4, 0), ("h3", 3, 0), ("h3", 3, 1), ("uA", 3), ("s3", 0), ("h2", 4, 1),
    ("tB", 3), ("h2", 4, 0), ("s2", 2), ("tA", 4), ("h4", 3, 1), ("h4", 3, 0), ("uB", 3),
    ("h3", 4, 1), ("tC", 3), ("uA", 4), ("h3", 4, 0), ("tB", 4), ("uC", 3), ("wg", 2),
    ("h4", 4, 1), ("h4", 4, 0), ("uB", 4), ("tC", 4), ("uC", 4), ("wg", 3), ("s3", 1),
    ("s2", 3), ("s2", 4), ("s3", 3), ("wg", 4), ("s3", 2), ("s3", 4),
)


def kernel(
    tok_hbm, cot_hbm, wg_hbm, wu_hbm, wd_hbm,
    gtok_hbm, gwg_hbm, gwu_hbm, gwd_hbm,
    xy, wgu, wd, part, rsend, rrecv, hid, gx, keep, dsend, drecv, bsend, brecv, asend, arecv,
    gtok, gwgu, gwd,
    ssem, rsem, lsem,
):
    r = lax.axis_index("row")
    c = lax.axis_index("col")
    core = lax.rem(c, 2)
    x = lax.rem(lax.div(c, 2), 4)
    y = lax.div(c, 8)
    a = x + core * (y - x)
    b = y + core * (x - y)

    def col(a_, b_):
        x_ = a_ + core * (b_ - a_)
        y_ = b_ + core * (a_ - b_)
        return y_ * 8 + x_ * 2 + core

    def m4(v):
        return lax.rem(v + 8, 4)

    def m8(v):
        return lax.rem(v + 16, 8)

    right = (m8(r + 1), c)
    left = (m8(r - 1), c)
    peer = (r, c + 1 - 2 * core)
    adev = {d: (r, col(m4(a + d), b)) for d in (1, 2, 3)}
    bdev = {d: (r, col(a, m4(b + d))) for d in (1, 2, 3)}
    place = core * 16 + b * 4 + a

    own_loads = [
        [
            pltpu.make_async_copy(
                src.at[pl.ds(s * RS, RS)], xy.at[s, place, k], lsem.at[2 * s + k]
            )
            for k, src in enumerate((tok_hbm, cot_hbm))
        ]
        for s in range(SLABS)
    ]
    weight_loads = [pltpu.make_async_copy(wd_hbm, wd, lsem.at[10])]
    for f in range(2):
        for k, src in enumerate((wg_hbm, wu_hbm)):
            weight_loads.append(
                pltpu.make_async_copy(
                    src.at[:, pl.ds(f * FH, FH)],
                    wgu.at[:, pl.ds((2 * f + k) * FH, FH)],
                    lsem.at[11 + 2 * f + k],
                )
            )
    for cp in sum(own_loads, []) + weight_loads:
        cp.start()

    barrier = pltpu.get_barrier_semaphore()
    partners = [right, left, peer] + [adev[d] for d in (1, 2, 3)] + [bdev[d] for d in (1, 2, 3)]
    for dev in partners:
        pl.semaphore_signal(barrier, inc=1, device_id=dev, device_id_type=MESH)
    pl.semaphore_wait(barrier, len(partners))

    sent = []

    def copy(src, dst, s, k, dev):
        return pltpu.make_async_remote_copy(
            src_ref=src, dst_ref=dst, send_sem=ssem.at[s, k], recv_sem=rsem.at[s, k],
            device_id=dev, device_id_type=MESH,
        )

    def send(src, dst, s, k, dev):
        cp = copy(src, dst, s, k, dev)
        cp.start()
        sent.append(cp)

    def recv(dst, s, k):
        copy(dst, dst, s, k, right).wait_recv()

    def pos(s, co, b_, a_):
        return xy.at[s, pl.ds(co * 16 + b_ * 4 + a_, 1)]

    def line(s, co, b_):
        return xy.at[s, pl.ds(co * 16 + b_ * 4, 4)]

    def chunk(ref, z, j, lo=0, n=CH):
        return ref.at[z, pl.ds(pl.multiple_of(j * CH + lo, 32), n)]

    def gather0(s):
        for cp in own_loads[s]:
            cp.wait()
        me = pos(s, core, b, a)
        for d in (1, 2, 3):
            send(me, me, s, A_A + d - 1, adev[d])

    def gather1(s):
        for d in (1, 2, 3):
            recv(pos(s, core, b, m4(a - d)), s, A_A + d - 1)
        row = line(s, core, b)
        for d in (1, 2, 3):
            send(row, row, s, A_B + d - 1, bdev[d])
        send(row, row, s, A_D, peer)

    def gather2(s):
        for d in (1, 3, 2):
            row = line(s, core, m4(b - d))
            recv(row, s, A_B + d - 1)
            send(row, row, s, A_D + d, peer)

    def project(s, f):
        z = 2 * s + f
        if f == 0:
            for d in range(4):
                recv(line(s, 1 - core, m4(a - d)), s, A_D + d)
            if s == 0:
                for cp in weight_loads:
                    cp.wait()
        xs = xy[s, :, 0].reshape(32 * RS, W)
        ys = xy[s, :, 1].reshape(32 * RS, W)
        part[z, :, 0 : 2 * FH] = jnp.dot(
            xs, wgu[:, 2 * FH * f : 2 * FH * (f + 1)], preferred_element_type=F32
        )
        part[z, :, 2 * FH : ZW] = lax.dot_general(
            ys, wd[FH * f : FH * (f + 1)], (((1,), (1,)), ((), ())), preferred_element_type=F32
        )

    def reduce_step(s, f, h):
        z = 2 * s + f
        kr, kl = R_R + 4 * f, R_L + 4 * f
        if h == 0:
            far = m8(r + 4)
            rsend[z, 0, 0, 0:HALF] = enc4(chunk(part, z, far, 0, HALF)[...])
            rsend[z, 1, 0, 0:HALF] = enc4(chunk(part, z, far, HALF, HALF)[...])
            for way, dev, k in ((0, right, kr), (1, left, kl)):
                send(
                    rsend.at[z, way, 0, pl.ds(0, HALF)],
                    rrecv.at[z, way, 0, pl.ds(0, HALF)],
                    s, k, dev,
                )
            return
        for way, dev, k, j in ((0, right, kr, m8(r + 4 - h)), (1, left, kl, m8(r - 4 + h))):
            if h == 1:
                got = rrecv.at[z, way, 0, pl.ds(0, HALF)]
                recv(got, s, k)
                near, rest = (0, HALF) if way == 0 else (HALF, 0)
                rsend[z, way, 1, near : near + HALF] = enc4(
                    chunk(part, z, j, near, HALF)[...] + dec4(got[...])
                )
                rsend[z, way, 1, rest : rest + HALF] = enc4(chunk(part, z, j, rest, HALF)[...])
            else:
                got = rrecv.at[z, way, h - 1]
                recv(got, s, k + h - 1)
                rsend[z, way, h] = enc4(chunk(part, z, j)[...] + dec4(got[...]))
            send(rsend.at[z, way, h], rrecv.at[z, way, h], s, k + h, dev)

    def activate(s, f):
        z = 2 * s + f
        recv(rrecv.at[z, 0, 3], s, R_R + 4 * f + 3)
        recv(rrecv.at[z, 1, 3], s, R_L + 4 * f + 3)
        mine = chunk(part, z, r)
        total = mine[...] + dec4(rrecv[z, 0, 3]) + dec4(rrecv[z, 1, 3])
        g, u, gh = total[:, 0:FH], total[:, FH : 2 * FH], total[:, 2 * FH :]
        sg = jax.nn.sigmoid(g)
        silu = g * sg
        out = chunk(hid, z, r)
        out[:, 0:FH] = (gh * u * sg * (1.0 + g * (1.0 - sg))).astype(BF)
        out[:, FH : 2 * FH] = (gh * silu).astype(BF)
        out[:, 2 * FH :] = (silu * u).astype(BF)

    def spread_step(s, f, h):
        z = 2 * s + f
        kr, kl = G_R + 4 * f, G_L + 4 * f
        if h == 0:
            activate(s, f)
            mine = chunk(hid, z, r)
            send(mine, mine, s, kr, right)
            send(mine, mine, s, kl, left)
            return
        if h <= 3:
            lo, hi = chunk(hid, z, m8(r - h)), chunk(hid, z, m8(r + h))
            recv(lo, s, kr + h - 1)
            if h == 3:
                half = chunk(hid, z, m8(r - 3), 0, HALF)
                send(half, half, s, kr + 3, right)
            else:
                send(lo, lo, s, kr + h, right)
            recv(hi, s, kl + h - 1)
            if h == 3:
                half = chunk(hid, z, m8(r + 3), HALF, HALF)
                send(half, half, s, kl + 3, left)
            else:
                send(hi, hi, s, kl + h, left)
            return
        recv(chunk(hid, z, m8(r + 4), 0, HALF), s, kr + 3)
        recv(chunk(hid, z, m8(r + 4), HALF, HALF), s, kl + 3)

    order = [m4(r + 2), m4(r + 1), m4(r + 3), m4(r)]

    def token_grad(s, i):
        def rows_of(co):
            j = co * 4 + order[i]
            both = [chunk(hid, 2 * s + f, j)[:, 0 : 2 * FH] for f in range(2)]
            return lax.dot_general(
                jnp.concatenate(both, axis=1), wgu[...], (((1,), (1,)), ((), ())),
                preferred_element_type=F32,
            )

        dsend[s, i] = enc2(rows_of(1 - core))
        send(dsend.at[s, i], drecv.at[s, i], s, S_D + i, peer)
        gx[s % 2, i] = rows_of(core)

    def add_peer(s, i):
        recv(drecv.at[s, i], s, S_D + i)
        total = gx[s % 2, i] + dec2(drecv[s, i])
        d = m4(order[i] - b)

        @pl.when(d == 0)
        def _():
            keep[s % 2] = total

        @pl.when(d != 0)
        def _():
            bsend[s, i] = enc2(total)
            copy(
                bsend.at[s, i], brecv.at[s, d - 1], s, S_B + d - 1, (r, col(a, order[i]))
            ).start()

    def weight_grads(s):
        xs = xy[s, :, 0].reshape(32 * RS, W)
        ys = xy[s, :, 1].reshape(32 * RS, W)
        over = (((0,), (0,)), ((), ()))
        gu = jnp.concatenate([hid[2 * s + f, :, 0 : 2 * FH] for f in range(2)], axis=1)
        hd = jnp.concatenate([hid[2 * s + f, :, 2 * FH :] for f in range(2)], axis=1)
        dgu = lax.dot_general(xs, gu, over, preferred_element_type=F32)
        dd = lax.dot_general(hd, ys, over, preferred_element_type=F32)
        if s == 0:
            gwgu[...] = dgu
            gwd[...] = dd
        else:
            gwgu[...] += dgu
            gwd[...] += dd

    def scatter2(s):
        total = keep[s % 2]
        for d in (1, 2, 3):
            recv(brecv.at[s, d - 1], s, S_B + d - 1)
            total = total + dec2(brecv[s, d - 1])
        keep[s % 2] = total
        for d in (1, 2, 3):
            rows = pl.ds(pl.multiple_of(m4(a + d) * RS, RS), RS)
            asend[s, d - 1] = enc2(keep[s % 2, rows])
            send(asend.at[s, d - 1], arecv.at[s, d - 1], s, S_A + d - 1, adev[d])
        gtok[s * RS : (s + 1) * RS] = keep[s % 2, pl.ds(pl.multiple_of(a * RS, RS), RS)]

    def scatter3(s):
        total = gtok[s * RS : (s + 1) * RS]
        for d in (1, 2, 3):
            recv(arecv.at[s, d - 1], s, S_A + d - 1)
            total = total + dec2(arecv[s, d - 1])
        gtok[s * RS : (s + 1) * RS] = total

    def run(name, s, f=0):
        if name[0] == "r":
            reduce_step(s, f, int(name[1]))
        elif name[0] == "h":
            spread_step(s, f, int(name[1]))
        elif name[0] == "t":
            for i in {"A": (0,), "B": (1, 2), "C": (3,)}[name[1]]:
                token_grad(s, i)
        elif name[0] == "u":
            for i in {"A": (0,), "B": (1, 2), "C": (3,)}[name[1]]:
                add_peer(s, i)
        elif name == "pj":
            project(s, f)
        else:
            {
                "g0": gather0, "g1": gather1, "g2": gather2,
                "wg": weight_grads, "s2": scatter2, "s3": scatter3,
            }[name](s)

    for step in ORDER:
        run(*step)

    stores = [
        pltpu.make_async_copy(gtok, gtok_hbm, lsem.at[0]),
        pltpu.make_async_copy(gwd, gwd_hbm, lsem.at[1]),
    ]
    for f in range(2):
        for k, dst in enumerate((gwg_hbm, gwu_hbm)):
            stores.append(
                pltpu.make_async_copy(
                    gwgu.at[:, pl.ds((2 * f + k) * FH, FH)],
                    dst.at[:, pl.ds(f * FH, FH)],
                    lsem.at[2 + 2 * f + k],
                )
            )
    for cp in stores:
        cp.start()
    for cp in sent:
        cp.wait_send()
    for s in range(SLABS):
        for d in (1, 2, 3):
            copy(bsend.at[s, 0], brecv.at[s, d - 1], s, S_B + d - 1, bdev[d]).wait_send()
    for cp in stores:
        cp.wait()


def write_out(*refs):
    ins, outs, bufs, sem_in, sem_out = refs[0:4], refs[4:8], refs[8:12], refs[12], refs[13]
    reads, writes = [], []
    for k, (src, buf, dst) in enumerate(zip(ins, bufs, outs)):
        n = src.shape[0] // 2
        for i in range(2):
            rows = pl.ds(i * n, n)
            reads.append(pltpu.make_async_copy(src.at[rows], buf.at[rows], sem_in.at[2 * k + i]))
            writes.append(pltpu.make_async_copy(buf.at[rows], dst.at[rows], sem_out.at[2 * k + i]))
    for cp in reads:
        cp.start()
    for rd, wr in zip(reads, writes):
        rd.wait()
        wr.start()
    for wr in writes:
        wr.wait()


def per_device(tokens, cotangent, gate_weight, up_weight, down_weight):
    hbm = pl.BlockSpec(memory_space=pl.ANY)
    rows = 32 * RS
    vm = pltpu.VMEM
    outs = pl.pallas_call(
        kernel,
        out_shape=(
            jax.ShapeDtypeStruct((SLABS * RS, W), F32),
            jax.ShapeDtypeStruct((W, H), F32),
            jax.ShapeDtypeStruct((W, H), F32),
            jax.ShapeDtypeStruct((H, W), F32),
        ),
        in_specs=[hbm] * 5,
        out_specs=[hbm] * 4,
        scratch_shapes=[
            vm((SLABS, 32, 2, RS, W), BF),
            vm((W, 2 * H), BF),
            vm((H, W), BF),
            vm((2 * SLABS, rows, ZW), F32),
            vm((2 * SLABS, 2, 4, CH, ZW), BF),
            vm((2 * SLABS, 2, 4, CH, ZW), BF),
            vm((2 * SLABS, rows, ZW), BF),
            vm((2, 4, CH, W), F32),
            vm((2, CH, W), F32),
            vm((SLABS, 4, CH, W), BF),
            vm((SLABS, 4, CH, W), BF),
            vm((SLABS, 4, CH, W), BF),
            vm((SLABS, 3, CH, W), BF),
            vm((SLABS, 3, RS, W), BF),
            vm((SLABS, 3, RS, W), BF),
            vm((SLABS * RS, W), F32),
            vm((W, 2 * H), F32),
            vm((H, W), F32),
            pltpu.SemaphoreType.DMA((SLABS, NSEM)),
            pltpu.SemaphoreType.DMA((SLABS, NSEM)),
            pltpu.SemaphoreType.DMA((15,)),
        ],
        compiler_params=pltpu.CompilerParams(
            collective_id=0, has_side_effects=True, vmem_limit_bytes=61 * 2**20
        ),
        name="swiglu_backward",
    )(tokens, cotangent, gate_weight, up_weight, down_weight)
    return pl.pallas_call(
        write_out,
        out_shape=[jax.ShapeDtypeStruct(o.shape, o.dtype) for o in outs],
        in_specs=[hbm] * 4,
        out_specs=[hbm] * 4,
        scratch_shapes=[vm(o.shape, o.dtype) for o in outs]
        + [pltpu.SemaphoreType.DMA((8,)), pltpu.SemaphoreType.DMA((8,))],
        name="write_out",
    )(*outs)


def solution(mesh):
    in_specs = (P("col", "row"), P("col", "row"), P("row", "col"), P("row", "col"), P("col", "row"))
    out_specs = (P("col", "row"), P("row", "col"), P("row", "col"), P("col", "row"))
    return jax.shard_map(
        per_device, mesh=mesh, in_specs=in_specs, out_specs=out_specs, check_vma=False
    )
```

```python
import jax
import jax.numpy as jnp
from jax import lax
from jax.experimental import pallas as pl
from jax.experimental.pallas import tpu as pltpu
from jax.sharding import PartitionSpec as P

MESH = pl.DeviceIdType.MESH
BF = jnp.bfloat16
F32 = jnp.float32

SLABS = 5
RS = 16
W = 640
H = 256
CH = 64
HALF = 32

ZW = 3 * H

SUM_PARTS = (((0, 2 * H), (2 * H, H)), ((0, 2 * H), (2 * H, H)), ((0, 2 * H), (2 * H, H)), ((0, 2 * H), (2 * H, H)), ((0, 2 * H), (2 * H, H)))
GATHER_PARTS = (((0, ZW // 2), (ZW // 2, ZW // 2)), ((0, ZW // 2), (ZW // 2, ZW // 2)), ((0, ZW // 2), (ZW // 2, ZW // 2)), ((0, ZW // 2), (ZW // 2, ZW // 2)), ((0, ZW // 2), (ZW // 2, ZW // 2)))
BY_LINE = (False,) * 4 + (True,)
PASSES = (4,) + (1,) * 4

A_A, A_B, A_D = 0, 3, 6
S_D, S_B, S_A = 10, 14, 17
R_R, R_L = 20, 28
G_R, G_L = 36, 44
Y_0 = 52
NSEM = 62


def enc4(v):
    t = v * jnp.abs(v) * (2.0**40)
    return (t * jnp.abs(t)).astype(BF)


def dec4(w):
    w = w.astype(F32)
    a = jnp.maximum(jnp.abs(w), 1e-37)
    r = lax.rsqrt(a)
    return (w * r) * (lax.rsqrt(a * r) * (2.0**-20))


def enc2(v):
    return (v * jnp.abs(v)).astype(BF)


def dec2(w):
    w = w.astype(F32)
    return w * lax.rsqrt(jnp.maximum(jnp.abs(w), 1e-37))


ORDER = (
    ("g0x", 0), ("g0y", 0), ("g0", 2), ("g0", 1), ("g1x", 0), ("g1y", 0), ("g1", 1), ("g1", 2),
    ("g2x", 0), ("g2y", 0), ("pj", 0, 0), ("r0", 0, 0), ("g2", 1), ("pj", 0, 1), ("r0", 0, 1),
    ("g0", 3), ("r1", 0, 0), ("r1", 0, 1), ("g2", 2), ("pj", 1, 0), ("r0", 1, 0), ("r2", 0, 0),
    ("pj", 1, 1), ("r0", 1, 1), ("g1", 3), ("r2", 0, 1), ("r1", 1, 0), ("pj", 2, 0),
    ("r0", 2, 0), ("g0", 4), ("r3", 0, 0), ("pj", 2, 1), ("r1", 1, 1), ("r3", 0, 1), ("g2", 3),
    ("r0", 2, 1), ("r1", 2, 0), ("r2", 1, 0), ("g1", 4), ("r2", 1, 1), ("ac", 0), ("r1", 2, 1),
    ("h0", 0, 0), ("pj", 3, 1), ("r0", 3, 1), ("r2", 2, 0), ("r3", 1, 0), ("r2", 2, 1),
    ("r3", 1, 1), ("pj", 3, 0), ("h1", 0, 0), ("h0", 0, 1), ("r3", 2, 0), ("r1", 3, 1),
    ("ac", 1), ("g2", 4), ("r0", 3, 0), ("r3", 2, 1), ("h2", 0, 0), ("h1", 0, 1), ("h0", 1, 1),
    ("h0", 1, 0), ("pj", 4, 1), ("h3", 0, 0), ("r1", 3, 0), ("pj", 4, 0), ("ac", 2),
    ("r0", 4, 0), ("r2", 3, 1), ("h4", 0, 0), ("h2", 0, 1), ("r0", 4, 1), ("h1", 1, 0),
    ("r2", 3, 0), ("h1", 1, 1), ("h3", 0, 1), ("r1", 4, 1), ("h0", 2, 1), ("h2", 1, 0),
    ("h0", 2, 0), ("h4", 0, 1), ("r3", 3, 0), ("h2", 1, 1), ("r1", 4, 0), ("r3", 3, 1),
    ("r2", 4, 1), ("wg", 0), ("h1", 2, 0), ("h3", 1, 1), ("tM", 0), ("h1", 2, 1), ("ac", 3),
    ("r2", 4, 0), ("h3", 1, 0), ("uM", 0), ("h2", 2, 0), ("h4", 1, 1), ("h2", 2, 1),
    ("r3", 4, 1), ("h0", 3, 1), ("h0", 3, 0), ("h4", 1, 0), ("tM", 1), ("r3", 4, 0), ("s2", 0),
    ("h3", 2, 1), ("wg", 1), ("h3", 2, 0), ("h1", 3, 1), ("h1", 3, 0), ("ac", 4), ("h4", 2, 1),
    ("h0", 4, 1), ("h0", 4, 0), ("h4", 2, 0), ("tM", 2), ("h2", 3, 1), ("uM", 1), ("h2", 3, 0),
    ("h1", 4, 1), ("uM", 2), ("h1", 4, 0), ("wg", 2), ("h3", 3, 1), ("h3", 3, 0), ("h2", 4, 1),
    ("s2", 1), ("h2", 4, 0), ("h4", 3, 1), ("h4", 3, 0), ("tM", 3), ("s2", 2), ("h3", 4, 1),
    ("h3", 4, 0), ("tA", 4), ("tB", 4), ("uM", 3), ("h4", 4, 1), ("uA", 4), ("h4", 4, 0),
    ("tC", 4), ("uB", 4), ("s3", 2), ("uC", 4), ("s3", 0), ("wg", 3), ("s2", 3), ("s2", 4),
    ("s3", 1), ("wg", 4), ("s3", 3), ("s3", 4),
)


def kernel(
    tok_hbm, cot_hbm, wg_hbm, wu_hbm, wd_hbm,
    gtok_hbm, gwg_hbm, gwu_hbm, gwd_hbm,
    xy, wgu, wd, part, rsend, rrecv, hid, gx, keep, dsend, drecv, bsend, brecv, asend, arecv,
    gtok, gwgu, gwd,
    ssem, rsem, lsem,
):
    r = lax.axis_index("row")
    c = lax.axis_index("col")
    core = lax.rem(c, 2)
    x = lax.rem(lax.div(c, 2), 4)
    y = lax.div(c, 8)
    a = x + core * (y - x)
    b = y + core * (x - y)

    def col(a_, b_):
        x_ = a_ + core * (b_ - a_)
        y_ = b_ + core * (a_ - b_)
        return y_ * 8 + x_ * 2 + core

    def m4(v):
        return lax.rem(v + 8, 4)

    def m8(v):
        return lax.rem(v + 16, 8)

    right = (m8(r + 1), c)
    left = (m8(r - 1), c)
    peer = (r, c + 1 - 2 * core)
    adev = {d: (r, col(m4(a + d), b)) for d in (1, 2, 3)}
    bdev = {d: (r, col(a, m4(b + d))) for d in (1, 2, 3)}
    place = core * 16 + b * 4 + a

    own_loads = [
        [
            pltpu.make_async_copy(
                src.at[pl.ds(s * RS, RS)], xy.at[s, place, k], lsem.at[2 * s + k]
            )
            for k, src in enumerate((tok_hbm, cot_hbm))
        ]
        for s in range(SLABS)
    ]
    weight_loads = [
        pltpu.make_async_copy(wg_hbm, wgu.at[:, pl.ds(0, H)], lsem.at[10]),
        pltpu.make_async_copy(wu_hbm, wgu.at[:, pl.ds(H, H)], lsem.at[11]),
        pltpu.make_async_copy(wd_hbm, wd, lsem.at[12]),
    ]
    for cp in sum(own_loads, []) + weight_loads:
        cp.start()

    barrier = pltpu.get_barrier_semaphore()
    partners = [right, left, peer] + [adev[d] for d in (1, 2, 3)] + [bdev[d] for d in (1, 2, 3)]
    for dev in partners:
        pl.semaphore_signal(barrier, inc=1, device_id=dev, device_id_type=MESH)
    pl.semaphore_wait(barrier, len(partners))

    sent = []

    def copy(src, dst, s, k, dev):
        return pltpu.make_async_remote_copy(
            src_ref=src, dst_ref=dst, send_sem=ssem.at[s, k], recv_sem=rsem.at[s, k],
            device_id=dev, device_id_type=MESH,
        )

    def send(src, dst, s, k, dev):
        cp = copy(src, dst, s, k, dev)
        cp.start()
        sent.append(cp)

    def recv(dst, s, k):
        copy(dst, dst, s, k, right).wait_recv()

    def pos(s, co, b_, a_, n=1, tag=""):
        at = pl.ds(co * 16 + b_ * 4 + a_, n)
        return xy.at[s, at, "xy".index(tag)] if tag else xy.at[s, at]

    def line(s, co, b_, tag=""):
        return pos(s, co, b_, 0, 4, tag)

    def chunk(ref, z, j, lo=0, n=CH):
        return ref.at[z, pl.ds(pl.multiple_of(j * CH + lo, 32), n)]

    def gather0(s, tag):
        k = Y_0 if tag == "y" else 0
        for cp in own_loads[s]["xy".index(tag) :][:1] if tag else own_loads[s]:
            cp.wait()
        me = pos(s, core, b, a, 1, tag)
        for d in (1, 2, 3):
            send(me, me, s, k + A_A + d - 1, adev[d])

    def gather1(s, tag):
        k = Y_0 if tag == "y" else 0
        for d in (1, 2, 3):
            recv(pos(s, core, b, m4(a - d), 1, tag), s, k + A_A + d - 1)
        row = line(s, core, b, tag)
        for d in (1, 2, 3):
            send(row, row, s, k + A_B + d - 1, bdev[d])
        if PASSES[s] == 4:
            send(row, row, s, k + A_D, peer)

    def half_of(s, co):
        return pos(s, co, 0, 0, 16)

    def gather2(s, tag):
        k = Y_0 if tag == "y" else 0
        for d in (1, 3, 2):
            row = line(s, core, m4(b - d), tag)
            recv(row, s, k + A_B + d - 1)
            if PASSES[s] == 4:
                send(row, row, s, k + A_D + d, peer)
        if PASSES[s] == 1:
            send(half_of(s, core), half_of(s, core), s, k + A_D, peer)

    ready = set()

    def project(s, f, both):
        first = s == 0 or s not in ready
        ready.add(s)
        for d in range(4) if PASSES[s] == 4 and first else ():
            tag, k = ("xy"[f], Y_0 * f) if s == 0 else ("", 0)
            recv(line(s, 1 - core, m4(a - d), tag), s, k + A_D + d)
        if PASSES[s] == 1 and first:
            recv(half_of(s, 1 - core), s, A_D)
        if s == 0:
            for cp in weight_loads[2 * f : 2 + f]:
                cp.wait()
        if f == 0:
            xs = xy[s, :, 0].reshape(32 * RS, W)
            part[s, :, 0 : 2 * H] = jnp.dot(xs, wgu[...], preferred_element_type=F32)
        if f == 1 or both:
            ys = xy[s, :, 1].reshape(32 * RS, W)
            part[s, :, 2 * H : ZW] = lax.dot_general(
                ys, wd[...], (((1,), (1,)), ((), ())), preferred_element_type=F32
            )

    def reduce_step(s, f, h):
        kr, kl = R_R + 4 * f, R_L + 4 * f
        lo, n = SUM_PARTS[s][f]
        lanes, cut = pl.ds(lo, n), slice(lo, lo + n)

        def mine(j, at=0, m=CH):
            return chunk(part, s, j, at, m)[:, cut]

        if h == 0:
            far = m8(r + 4)
            for way, dev, k in ((0, right, kr), (1, left, kl)):
                rsend[s, way, 0, 0:HALF, cut] = enc4(mine(far, HALF * way, HALF))
                send(
                    rsend.at[s, way, 0, pl.ds(0, HALF), lanes],
                    rrecv.at[s, way, 0, pl.ds(0, HALF), lanes],
                    s, k, dev,
                )
            return
        for way, dev, k, j in ((0, right, kr, m8(r + 4 - h)), (1, left, kl, m8(r - 4 + h))):
            if h == 1:
                recv(rrecv.at[s, way, 0, pl.ds(0, HALF), lanes], s, k)
                near, rest = (0, HALF) if way == 0 else (HALF, 0)
                rsend[s, way, 1, near : near + HALF, cut] = enc4(
                    mine(j, near, HALF) + dec4(rrecv[s, way, 0, 0:HALF, cut])
                )
                rsend[s, way, 1, rest : rest + HALF, cut] = enc4(mine(j, rest, HALF))
            else:
                recv(rrecv.at[s, way, h - 1, :, lanes], s, k + h - 1)
                rsend[s, way, h, :, cut] = enc4(mine(j) + dec4(rrecv[s, way, h - 1, :, cut]))
            send(rsend.at[s, way, h, :, lanes], rrecv.at[s, way, h, :, lanes], s, k + h, dev)

    def activate(s):
        for f, (lo, n) in enumerate(SUM_PARTS[s]):
            recv(rrecv.at[s, 0, 3, :, pl.ds(lo, n)], s, R_R + 4 * f + 3)
            recv(rrecv.at[s, 1, 3, :, pl.ds(lo, n)], s, R_L + 4 * f + 3)
        total = chunk(part, s, r)[...] + dec4(rrecv[s, 0, 3]) + dec4(rrecv[s, 1, 3])
        g, u, gh = total[:, 0:H], total[:, H : 2 * H], total[:, 2 * H :]
        sg = jax.nn.sigmoid(g)
        silu = g * sg
        out = chunk(hid, s, r)
        out[:, 0:H] = (gh * u * sg * (1.0 + g * (1.0 - sg))).astype(BF)
        out[:, H : 2 * H] = (gh * silu).astype(BF)
        out[:, 2 * H :] = (silu * u).astype(BF)

    def spread_step(s, f, h):
        lo_lane, n_lane = GATHER_PARTS[s][f]

        def part_of(j, at=0, m=CH):
            rows = pl.ds(pl.multiple_of(j * CH + at, 32), m)
            return hid.at[s, rows, pl.ds(lo_lane, n_lane)]

        kr, kl = G_R + 4 * f, G_L + 4 * f
        if h == 0:
            mine = part_of(r)
            send(mine, mine, s, kr, right)
            send(mine, mine, s, kl, left)
            return
        if h <= 3:
            lo, hi = part_of(m8(r - h)), part_of(m8(r + h))
            recv(lo, s, kr + h - 1)
            if h == 3:
                half = part_of(m8(r - 3), 0, HALF)
                send(half, half, s, kr + 3, right)
            else:
                send(lo, lo, s, kr + h, right)
            recv(hi, s, kl + h - 1)
            if h == 3:
                half = part_of(m8(r + 3), HALF, HALF)
                send(half, half, s, kl + 3, left)
            else:
                send(hi, hi, s, kl + h, left)
            return
        recv(part_of(m8(r + 4), 0, HALF), s, kr + 3)
        recv(part_of(m8(r + 4), HALF, HALF), s, kl + 3)

    order = [m4(r + 2), m4(r + 1), m4(r + 3), m4(r)]

    def token_grad(s, i):
        def rows_of(co):
            return lax.dot_general(
                chunk(hid, s, co * 4 + order[i])[:, 0 : 2 * H], wgu[...],
                (((1,), (1,)), ((), ())), preferred_element_type=F32,
            )

        dsend[s, i] = enc2(rows_of(1 - core))
        send(dsend.at[s, i], drecv.at[s, i], s, S_D + i, peer)
        gx[s % 2, i] = rows_of(core)

    def add_peer(s, i):
        recv(drecv.at[s, i], s, S_D + i)
        total = gx[s % 2, i] + dec2(drecv[s, i])
        d = m4(order[i] - b)

        @pl.when(d == 0)
        def _():
            keep[s % 2] = total

        @pl.when(d != 0)
        def _():
            bsend[s, i] = enc2(total)
            copy(
                bsend.at[s, i], brecv.at[s, d - 1], s, S_B + d - 1, (r, col(a, order[i]))
            ).start()

    def token_grad_whole(s):
        for co in (1 - core, core):
            rows = pl.ds(pl.multiple_of(co * 256, 256), 256)
            gx[s % 2] = lax.dot_general(
                hid[s, rows, 0 : 2 * H], wgu[...], (((1,), (1,)), ((), ())),
                preferred_element_type=F32,
            ).reshape(4, CH, W)
            if co is not core:
                dsend[s] = enc2(gx[s % 2])
                send(dsend.at[s], drecv.at[s], s, S_D, peer)

    def add_peer_whole(s):
        recv(drecv.at[s], s, S_D)
        gx[s % 2] = gx[s % 2] + dec2(drecv[s])
        for d in (1, 2, 3):
            bsend[s, d] = enc2(gx[s % 2, m4(b + d)])
            send(bsend.at[s, d], brecv.at[s, d - 1], s, S_B + d - 1, bdev[d])
        keep[s % 2] = gx[s % 2, b]

    def weight_grads(s):
        xs = xy[s, :, 0].reshape(32 * RS, W)
        ys = xy[s, :, 1].reshape(32 * RS, W)
        over = (((0,), (0,)), ((), ()))
        gu, hd = hid[s, :, 0 : 2 * H], hid[s, :, 2 * H :]
        dgu = lax.dot_general(xs, gu, over, preferred_element_type=F32)
        dd = lax.dot_general(hd, ys, over, preferred_element_type=F32)
        if s == 0:
            gwgu[...] = dgu
            gwd[...] = dd
        else:
            gwgu[...] += dgu
            gwd[...] += dd

    def scatter2(s):
        total = keep[s % 2]
        for d in (1, 2, 3):
            recv(brecv.at[s, d - 1], s, S_B + d - 1)
            total = total + dec2(brecv[s, d - 1])
        keep[s % 2] = total
        for d in (1, 2, 3):
            rows = pl.ds(pl.multiple_of(m4(a + d) * RS, RS), RS)
            asend[s, d - 1] = enc2(keep[s % 2, rows])
            send(asend.at[s, d - 1], arecv.at[s, d - 1], s, S_A + d - 1, adev[d])
        gtok[s * RS : (s + 1) * RS] = keep[s % 2, pl.ds(pl.multiple_of(a * RS, RS), RS)]

    def scatter3(s):
        total = gtok[s * RS : (s + 1) * RS]
        for d in (1, 2, 3):
            recv(arecv.at[s, d - 1], s, S_A + d - 1)
            total = total + dec2(arecv[s, d - 1])
        gtok[s * RS : (s + 1) * RS] = total

    def run(name, s, f=0):
        if name[0] == "r":
            reduce_step(s, f, int(name[1]))
        elif name[0] == "h":
            spread_step(s, f, int(name[1]))
        elif name in ("tM", "uM"):
            (token_grad_whole if name == "tM" else add_peer_whole)(s)
        elif name[0] == "t":
            for i in {"A": (0,), "B": (1, 2), "C": (3,)}[name[1]]:
                token_grad(s, i)
        elif name[0] == "u":
            for i in {"A": (0,), "B": (1, 2), "C": (3,)}[name[1]]:
                add_peer(s, i)
        elif name == "pj":
            project(s, f, len(SUM_PARTS[s]) == 1)
        elif name[0] == "g":
            (gather0, gather1, gather2)[int(name[1])](s, name[2:])
        else:
            {
                "ac": activate, "wg": weight_grads, "s2": scatter2, "s3": scatter3,
            }[name](s)

    for step in ORDER:
        run(*step)

    stores = [
        pltpu.make_async_copy(gtok, gtok_hbm, lsem.at[0]),
        pltpu.make_async_copy(gwd, gwd_hbm, lsem.at[1]),
    ]
    for k, dst in enumerate((gwg_hbm, gwu_hbm)):
        stores.append(
            pltpu.make_async_copy(gwgu.at[:, pl.ds(k * H, H)], dst, lsem.at[2 + k])
        )
    for cp in stores:
        cp.start()
    for cp in sent:
        cp.wait_send()
    for s in range(SLABS):
        for d in (1, 2, 3) if BY_LINE[s] else ():
            copy(bsend.at[s, 0], brecv.at[s, d - 1], s, S_B + d - 1, bdev[d]).wait_send()
    for cp in stores:
        cp.wait()


def write_out(*refs):
    ins, outs, bufs, sem_in, sem_out = refs[0:4], refs[4:8], refs[8:12], refs[12], refs[13]
    reads, writes = [], []
    for k, (src, buf, dst) in enumerate(zip(ins, bufs, outs)):
        n = src.shape[0] // 2
        for i in range(2):
            rows = pl.ds(i * n, n)
            reads.append(pltpu.make_async_copy(src.at[rows], buf.at[rows], sem_in.at[2 * k + i]))
            writes.append(pltpu.make_async_copy(buf.at[rows], dst.at[rows], sem_out.at[2 * k + i]))
    for cp in reads:
        cp.start()
    for rd, wr in zip(reads, writes):
        rd.wait()
        wr.start()
    for wr in writes:
        wr.wait()


def per_device(tokens, cotangent, gate_weight, up_weight, down_weight):
    hbm = pl.BlockSpec(memory_space=pl.ANY)
    rows = 32 * RS
    vm = pltpu.VMEM
    outs = pl.pallas_call(
        kernel,
        out_shape=(
            jax.ShapeDtypeStruct((SLABS * RS, W), F32),
            jax.ShapeDtypeStruct((W, H), F32),
            jax.ShapeDtypeStruct((W, H), F32),
            jax.ShapeDtypeStruct((H, W), F32),
        ),
        in_specs=[hbm] * 5,
        out_specs=[hbm] * 4,
        scratch_shapes=[
            vm((SLABS, 32, 2, RS, W), BF),
            vm((W, 2 * H), BF),
            vm((H, W), BF),
            vm((SLABS, rows, ZW), F32),
            vm((SLABS, 2, 4, CH, ZW), BF),
            vm((SLABS, 2, 4, CH, ZW), BF),
            vm((SLABS, rows, ZW), BF),
            vm((2, 4, CH, W), F32),
            vm((2, CH, W), F32),
            vm((SLABS, 4, CH, W), BF),
            vm((SLABS, 4, CH, W), BF),
            vm((SLABS, 4, CH, W), BF),
            vm((SLABS, 3, CH, W), BF),
            vm((SLABS, 3, RS, W), BF),
            vm((SLABS, 3, RS, W), BF),
            vm((SLABS * RS, W), F32),
            vm((W, 2 * H), F32),
            vm((H, W), F32),
            pltpu.SemaphoreType.DMA((SLABS, NSEM)),
            pltpu.SemaphoreType.DMA((SLABS, NSEM)),
            pltpu.SemaphoreType.DMA((15,)),
        ],
        compiler_params=pltpu.CompilerParams(
            collective_id=0, has_side_effects=True, vmem_limit_bytes=61 * 2**20
        ),
        name="swiglu_backward",
    )(tokens, cotangent, gate_weight, up_weight, down_weight)
    return pl.pallas_call(
        write_out,
        out_shape=[jax.ShapeDtypeStruct(o.shape, o.dtype) for o in outs],
        in_specs=[hbm] * 4,
        out_specs=[hbm] * 4,
        scratch_shapes=[vm(o.shape, o.dtype) for o in outs]
        + [pltpu.SemaphoreType.DMA((8,)), pltpu.SemaphoreType.DMA((8,))],
        name="write_out",
    )(*outs)


def solution(mesh):
    in_specs = (P("col", "row"), P("col", "row"), P("row", "col"), P("row", "col"), P("col", "row"))
    out_specs = (P("col", "row"), P("row", "col"), P("row", "col"), P("col", "row"))
    return jax.shard_map(
        per_device, mesh=mesh, in_specs=in_specs, out_specs=out_specs, check_vma=False
    )
```

```python
import jax
import jax.numpy as jnp
from jax import lax
from jax.experimental import pallas as pl
from jax.experimental.pallas import tpu as pltpu
from jax.sharding import PartitionSpec as P

MESH = pl.DeviceIdType.MESH
BF = jnp.bfloat16
F32 = jnp.float32

SLABS = 5
RS = 16
W = 640
H = 256
CH = 64
HALF = 32

ZW = 3 * H

SUM_PARTS = (((0, 2 * H), (2 * H, H)), ((0, 2 * H), (2 * H, H)), ((0, 2 * H), (2 * H, H)), ((0, 2 * H), (2 * H, H)), ((0, 2 * H), (2 * H, H)))
GATHER_PARTS = (((0, ZW // 2), (ZW // 2, ZW // 2)), ((0, ZW // 2), (ZW // 2, ZW // 2)), ((0, ZW // 2), (ZW // 2, ZW // 2)), ((0, ZW // 2), (ZW // 2, ZW // 2)), ((0, ZW // 2), (ZW // 2, ZW // 2)))
BY_LINE = (False,) * 4 + (True,)
PASSES = (4,) + (1,) * 4

A_A, A_B, A_D = 0, 3, 6
S_D, S_B, S_A = 10, 14, 17
R_R, R_L = 20, 28
G_R, G_L = 36, 44
Y_0 = 52
NSEM = 62


def enc4(v):
    t = v * jnp.abs(v) * (2.0**40)
    return (t * jnp.abs(t)).astype(BF)


def dec4(w):
    w = w.astype(F32)
    a = jnp.maximum(jnp.abs(w), 1e-37)
    r = lax.rsqrt(a)
    return (w * r) * (lax.rsqrt(a * r) * (2.0**-20))


def enc2(v):
    return (v * jnp.abs(v)).astype(BF)


def dec2(w):
    w = w.astype(F32)
    return w * lax.rsqrt(jnp.maximum(jnp.abs(w), 1e-37))


ORDER = (
    ("g0x", 0), ("g0y", 0), ("g0", 2), ("g0", 1), ("g1x", 0), ("g1y", 0), ("g1", 1), ("g1", 2),
    ("g2x", 0), ("g2y", 0), ("pj", 0, 0), ("r0", 0, 0), ("g2", 1), ("pj", 0, 1), ("r0", 0, 1),
    ("g0", 3), ("r1", 0, 0), ("r1", 0, 1), ("g2", 2), ("pj", 1, 0), ("r0", 1, 0), ("r2", 0, 0),
    ("pj", 1, 1), ("r0", 1, 1), ("g1", 3), ("r2", 0, 1), ("r1", 1, 0), ("pj", 2, 0),
    ("r0", 2, 0), ("g0", 4), ("r3", 0, 0), ("pj", 2, 1), ("r1", 1, 1), ("r3", 0, 1), ("g2", 3),
    ("r0", 2, 1), ("r1", 2, 0), ("r2", 1, 0), ("g1", 4), ("r2", 1, 1), ("ac", 0), ("r1", 2, 1),
    ("h0", 0, 0), ("pj", 3, 1), ("r0", 3, 1), ("r2", 2, 0), ("r3", 1, 0), ("r2", 2, 1),
    ("r3", 1, 1), ("pj", 3, 0), ("h1", 0, 0), ("h0", 0, 1), ("r3", 2, 0), ("r1", 3, 1),
    ("ac", 1), ("g2", 4), ("r0", 3, 0), ("r3", 2, 1), ("h2", 0, 0), ("h1", 0, 1), ("h0", 1, 1),
    ("h0", 1, 0), ("pj", 4, 1), ("h3", 0, 0), ("r1", 3, 0), ("pj", 4, 0), ("ac", 2),
    ("r0", 4, 0), ("r2", 3, 1), ("h4", 0, 0), ("h2", 0, 1), ("r0", 4, 1), ("h1", 1, 0),
    ("r2", 3, 0), ("h1", 1, 1), ("h3", 0, 1), ("r1", 4, 1), ("h0", 2, 1), ("h2", 1, 0),
    ("h0", 2, 0), ("h4", 0, 1), ("r3", 3, 0), ("h2", 1, 1), ("r1", 4, 0), ("r3", 3, 1),
    ("r2", 4, 1), ("wg", 0), ("h1", 2, 0), ("h3", 1, 1), ("tM", 0), ("h1", 2, 1), ("ac", 3),
    ("r2", 4, 0), ("h3", 1, 0), ("uM", 0), ("h2", 2, 0), ("h4", 1, 1), ("h2", 2, 1),
    ("r3", 4, 1), ("h0", 3, 1), ("h0", 3, 0), ("h4", 1, 0), ("tM", 1), ("r3", 4, 0), ("s2", 0),
    ("h3", 2, 1), ("wg", 1), ("h3", 2, 0), ("h1", 3, 1), ("h1", 3, 0), ("ac", 4), ("h4", 2, 1),
    ("h0", 4, 1), ("h0", 4, 0), ("h4", 2, 0), ("tM", 2), ("h2", 3, 1), ("uM", 1), ("h2", 3, 0),
    ("h1", 4, 1), ("uM", 2), ("h1", 4, 0), ("wg", 2), ("h3", 3, 1), ("h3", 3, 0), ("h2", 4, 1),
    ("s2", 1), ("h2", 4, 0), ("h4", 3, 1), ("h4", 3, 0), ("tM", 3), ("s2", 2), ("h3", 4, 1),
    ("h3", 4, 0), ("tA", 4), ("tB", 4), ("uM", 3), ("h4", 4, 1), ("uA", 4), ("h4", 4, 0),
    ("tC", 4), ("uB", 4), ("s3", 2), ("uC", 4), ("s3", 0), ("wg", 3), ("s2", 3), ("s2", 4),
    ("s3", 1), ("wg", 4), ("s3", 3), ("s3", 4),
)


def kernel(
    tok_hbm, cot_hbm, wg_hbm, wu_hbm, wd_hbm,
    gtok_hbm, gwg_hbm, gwu_hbm, gwd_hbm,
    xy, wgu, wd, part, rsend, rrecv, hid, gx, keep, dsend, drecv, bsend, brecv, asend, arecv,
    gtok, gwgu, gwd,
    ssem, rsem, lsem,
):
    r = lax.axis_index("row")
    c = lax.axis_index("col")
    core = lax.rem(c, 2)
    x = lax.rem(lax.div(c, 2), 4)
    y = lax.div(c, 8)
    a = x + core * (y - x)
    b = y + core * (x - y)

    def col(a_, b_):
        x_ = a_ + core * (b_ - a_)
        y_ = b_ + core * (a_ - b_)
        return y_ * 8 + x_ * 2 + core

    def m4(v):
        return lax.rem(v + 8, 4)

    def m8(v):
        return lax.rem(v + 16, 8)

    right = (m8(r + 1), c)
    left = (m8(r - 1), c)
    peer = (r, c + 1 - 2 * core)
    adev = {d: (r, col(m4(a + d), b)) for d in (1, 2, 3)}
    bdev = {d: (r, col(a, m4(b + d))) for d in (1, 2, 3)}
    place = core * 16 + b * 4 + a

    own_loads = [
        [
            pltpu.make_async_copy(
                src.at[pl.ds(s * RS, RS)], xy.at[s, place, k], lsem.at[2 * s + k]
            )
            for k, src in enumerate((tok_hbm, cot_hbm))
        ]
        for s in range(SLABS)
    ]
    weight_loads = [
        pltpu.make_async_copy(wg_hbm, wgu.at[:, pl.ds(0, H)], lsem.at[10]),
        pltpu.make_async_copy(wu_hbm, wgu.at[:, pl.ds(H, H)], lsem.at[11]),
        pltpu.make_async_copy(wd_hbm, wd, lsem.at[12]),
    ]
    for cp in sum(own_loads, []) + weight_loads:
        cp.start()

    barrier = pltpu.get_barrier_semaphore()
    partners = [right, left, peer] + [adev[d] for d in (1, 2, 3)] + [bdev[d] for d in (1, 2, 3)]
    for dev in partners:
        pl.semaphore_signal(barrier, inc=1, device_id=dev, device_id_type=MESH)
    pl.semaphore_wait(barrier, len(partners))

    sent = []

    def copy(src, dst, s, k, dev):
        return pltpu.make_async_remote_copy(
            src_ref=src, dst_ref=dst, send_sem=ssem.at[s, k], recv_sem=rsem.at[s, k],
            device_id=dev, device_id_type=MESH,
        )

    def send(src, dst, s, k, dev):
        cp = copy(src, dst, s, k, dev)
        cp.start()
        sent.append(cp)

    def recv(dst, s, k):
        copy(dst, dst, s, k, right).wait_recv()

    def pos(s, co, b_, a_, n=1, tag=""):
        at = pl.ds(co * 16 + b_ * 4 + a_, n)
        return xy.at[s, at, "xy".index(tag)] if tag else xy.at[s, at]

    def line(s, co, b_, tag=""):
        return pos(s, co, b_, 0, 4, tag)

    def chunk(ref, z, j, lo=0, n=CH):
        return ref.at[z, pl.ds(pl.multiple_of(j * CH + lo, 32), n)]

    def gather0(s, tag):
        k = Y_0 if tag == "y" else 0
        for cp in own_loads[s]["xy".index(tag) :][:1] if tag else own_loads[s]:
            cp.wait()
        me = pos(s, core, b, a, 1, tag)
        for d in (1, 2, 3):
            send(me, me, s, k + A_A + d - 1, adev[d])

    def gather1(s, tag):
        k = Y_0 if tag == "y" else 0
        for d in (1, 2, 3):
            recv(pos(s, core, b, m4(a - d), 1, tag), s, k + A_A + d - 1)
        row = line(s, core, b, tag)
        for d in (1, 2, 3):
            send(row, row, s, k + A_B + d - 1, bdev[d])
        if PASSES[s] == 4:
            send(row, row, s, k + A_D, peer)

    def half_of(s, co):
        return pos(s, co, 0, 0, 16)

    def gather2(s, tag):
        k = Y_0 if tag == "y" else 0
        for d in (1, 3, 2):
            row = line(s, core, m4(b - d), tag)
            recv(row, s, k + A_B + d - 1)
            if PASSES[s] == 4:
                send(row, row, s, k + A_D + d, peer)
        if PASSES[s] == 1:
            send(half_of(s, core), half_of(s, core), s, k + A_D, peer)

    ready = set()

    def project(s, f, both):
        first = s == 0 or s not in ready
        ready.add(s)
        for d in range(4) if PASSES[s] == 4 and first else ():
            tag, k = ("xy"[f], Y_0 * f) if s == 0 else ("", 0)
            recv(line(s, 1 - core, m4(a - d), tag), s, k + A_D + d)
        if PASSES[s] == 1 and first:
            recv(half_of(s, 1 - core), s, A_D)
        if s == 0:
            for cp in weight_loads[2 * f : 2 + f]:
                cp.wait()
        if f == 0:
            xs = xy[s, :, 0].reshape(32 * RS, W)
            part[s, :, 0 : 2 * H] = jnp.dot(xs, wgu[...], preferred_element_type=F32)
        if f == 1 or both:
            ys = xy[s, :, 1].reshape(32 * RS, W)
            part[s, :, 2 * H : ZW] = lax.dot_general(
                ys, wd[...], (((1,), (1,)), ((), ())), preferred_element_type=F32
            )

    def reduce_step(s, f, h):
        kr, kl = R_R + 4 * f, R_L + 4 * f
        lo, n = SUM_PARTS[s][f]
        lanes, cut = pl.ds(lo, n), slice(lo, lo + n)

        def mine(j, at=0, m=CH):
            return chunk(part, s, j, at, m)[:, cut]

        if h == 0:
            far = m8(r + 4)
            for way, dev, k in ((0, right, kr), (1, left, kl)):
                rsend[s, way, 0, 0:HALF, cut] = enc4(mine(far, HALF * way, HALF))
                send(
                    rsend.at[s, way, 0, pl.ds(0, HALF), lanes],
                    rrecv.at[s, way, 0, pl.ds(0, HALF), lanes],
                    s, k, dev,
                )
            return
        for way, dev, k, j in ((0, right, kr, m8(r + 4 - h)), (1, left, kl, m8(r - 4 + h))):
            if h == 1:
                recv(rrecv.at[s, way, 0, pl.ds(0, HALF), lanes], s, k)
                near, rest = (0, HALF) if way == 0 else (HALF, 0)
                rsend[s, way, 1, near : near + HALF, cut] = enc4(
                    mine(j, near, HALF) + dec4(rrecv[s, way, 0, 0:HALF, cut])
                )
                rsend[s, way, 1, rest : rest + HALF, cut] = enc4(mine(j, rest, HALF))
            else:
                recv(rrecv.at[s, way, h - 1, :, lanes], s, k + h - 1)
                rsend[s, way, h, :, cut] = enc4(mine(j) + dec4(rrecv[s, way, h - 1, :, cut]))
            send(rsend.at[s, way, h, :, lanes], rrecv.at[s, way, h, :, lanes], s, k + h, dev)

    def activate(s):
        for f, (lo, n) in enumerate(SUM_PARTS[s]):
            recv(rrecv.at[s, 0, 3, :, pl.ds(lo, n)], s, R_R + 4 * f + 3)
            recv(rrecv.at[s, 1, 3, :, pl.ds(lo, n)], s, R_L + 4 * f + 3)
        total = chunk(part, s, r)[...] + dec4(rrecv[s, 0, 3]) + dec4(rrecv[s, 1, 3])
        g, u, gh = total[:, 0:H], total[:, H : 2 * H], total[:, 2 * H :]
        sg = jax.nn.sigmoid(g)
        silu = g * sg
        out = chunk(hid, s, r)
        out[:, 0:H] = (gh * u * sg * (1.0 + g * (1.0 - sg))).astype(BF)
        out[:, H : 2 * H] = (gh * silu).astype(BF)
        out[:, 2 * H :] = (silu * u).astype(BF)

    def spread_step(s, f, h):
        lo_lane, n_lane = GATHER_PARTS[s][f]

        def part_of(j, at=0, m=CH):
            rows = pl.ds(pl.multiple_of(j * CH + at, 32), m)
            return hid.at[s, rows, pl.ds(lo_lane, n_lane)]

        kr, kl = G_R + 4 * f, G_L + 4 * f
        if h == 0:
            mine = part_of(r)
            send(mine, mine, s, kr, right)
            send(mine, mine, s, kl, left)
            return
        if h <= 3:
            lo, hi = part_of(m8(r - h)), part_of(m8(r + h))
            recv(lo, s, kr + h - 1)
            if h == 3:
                half = part_of(m8(r - 3), 0, HALF)
                send(half, half, s, kr + 3, right)
            else:
                send(lo, lo, s, kr + h, right)
            recv(hi, s, kl + h - 1)
            if h == 3:
                half = part_of(m8(r + 3), HALF, HALF)
                send(half, half, s, kl + 3, left)
            else:
                send(hi, hi, s, kl + h, left)
            return
        recv(part_of(m8(r + 4), 0, HALF), s, kr + 3)
        recv(part_of(m8(r + 4), HALF, HALF), s, kl + 3)

    order = [m4(r + 2), m4(r + 1), m4(r + 3), m4(r)]

    def token_grad(s, i):
        def rows_of(co):
            return lax.dot_general(
                chunk(hid, s, co * 4 + order[i])[:, 0 : 2 * H], wgu[...],
                (((1,), (1,)), ((), ())), preferred_element_type=F32,
            )

        dsend[s, i] = enc2(rows_of(1 - core))
        send(dsend.at[s, i], drecv.at[s, i], s, S_D + i, peer)
        gx[s % 2, i] = rows_of(core)

    def add_peer(s, i):
        recv(drecv.at[s, i], s, S_D + i)
        total = gx[s % 2, i] + dec2(drecv[s, i])
        d = m4(order[i] - b)

        @pl.when(d == 0)
        def _():
            keep[s % 2] = total

        @pl.when(d != 0)
        def _():
            bsend[s, i] = enc2(total)
            copy(
                bsend.at[s, i], brecv.at[s, d - 1], s, S_B + d - 1, (r, col(a, order[i]))
            ).start()

    def token_grad_whole(s):
        for co in (1 - core, core):
            rows = pl.ds(pl.multiple_of(co * 256, 256), 256)
            gx[s % 2] = lax.dot_general(
                hid[s, rows, 0 : 2 * H], wgu[...], (((1,), (1,)), ((), ())),
                preferred_element_type=F32,
            ).reshape(4, CH, W)
            if co is not core:
                dsend[s] = enc2(gx[s % 2])
                send(dsend.at[s], drecv.at[s], s, S_D, peer)

    def add_peer_whole(s):
        recv(drecv.at[s], s, S_D)
        gx[s % 2] = gx[s % 2] + dec2(drecv[s])
        for d in (1, 2, 3):
            bsend[s, d] = enc2(gx[s % 2, m4(b + d)])
            send(bsend.at[s, d], brecv.at[s, d - 1], s, S_B + d - 1, bdev[d])
        keep[s % 2] = gx[s % 2, b]

    def weight_grads(s):
        xs = xy[s, :, 0].reshape(32 * RS, W)
        ys = xy[s, :, 1].reshape(32 * RS, W)
        over = (((0,), (0,)), ((), ()))
        gu, hd = hid[s, :, 0 : 2 * H], hid[s, :, 2 * H :]
        dgu = lax.dot_general(xs, gu, over, preferred_element_type=F32)
        dd = lax.dot_general(hd, ys, over, preferred_element_type=F32)
        if s == 0:
            gwgu[...] = dgu
            gwd[...] = dd
        else:
            gwgu[...] += dgu
            gwd[...] += dd

    def scatter2(s):
        total = keep[s % 2]
        for d in (1, 2, 3):
            recv(brecv.at[s, d - 1], s, S_B + d - 1)
            total = total + dec2(brecv[s, d - 1])
        keep[s % 2] = total
        for d in (1, 2, 3):
            rows = pl.ds(pl.multiple_of(m4(a + d) * RS, RS), RS)
            asend[s, d - 1] = enc2(keep[s % 2, rows])
            send(asend.at[s, d - 1], arecv.at[s, d - 1], s, S_A + d - 1, adev[d])
        gtok[s * RS : (s + 1) * RS] = keep[s % 2, pl.ds(pl.multiple_of(a * RS, RS), RS)]

    def scatter3(s):
        total = gtok[s * RS : (s + 1) * RS]
        for d in (1, 2, 3):
            recv(arecv.at[s, d - 1], s, S_A + d - 1)
            total = total + dec2(arecv[s, d - 1])
        gtok[s * RS : (s + 1) * RS] = total

    def run(name, s, f=0):
        if name[0] == "r":
            reduce_step(s, f, int(name[1]))
        elif name[0] == "h":
            spread_step(s, f, int(name[1]))
        elif name in ("tM", "uM"):
            (token_grad_whole if name == "tM" else add_peer_whole)(s)
        elif name[0] == "t":
            for i in {"A": (0,), "B": (1, 2), "C": (3,)}[name[1]]:
                token_grad(s, i)
        elif name[0] == "u":
            for i in {"A": (0,), "B": (1, 2), "C": (3,)}[name[1]]:
                add_peer(s, i)
        elif name == "pj":
            project(s, f, len(SUM_PARTS[s]) == 1)
        elif name[0] == "g":
            (gather0, gather1, gather2)[int(name[1])](s, name[2:])
        else:
            {
                "ac": activate, "wg": weight_grads, "s2": scatter2, "s3": scatter3,
            }[name](s)

    weight_stores = [
        pltpu.make_async_copy(gwd, gwd_hbm, lsem.at[1]),
        pltpu.make_async_copy(gwgu.at[:, pl.ds(0, H)], gwg_hbm, lsem.at[2]),
        pltpu.make_async_copy(gwgu.at[:, pl.ds(H, H)], gwu_hbm, lsem.at[3]),
    ]
    for step in ORDER:
        run(*step)
        if step == ("wg", SLABS - 1):
            for cp in weight_stores:
                cp.start()

    token_store = pltpu.make_async_copy(gtok, gtok_hbm, lsem.at[0])
    token_store.start()
    for cp in sent:
        cp.wait_send()
    for s in range(SLABS):
        for d in (1, 2, 3) if BY_LINE[s] else ():
            copy(bsend.at[s, 0], brecv.at[s, d - 1], s, S_B + d - 1, bdev[d]).wait_send()
    for cp in weight_stores + [token_store]:
        cp.wait()


def write_out(*refs):
    ins, outs, bufs, sem_in, sem_out = refs[0:4], refs[4:8], refs[8:12], refs[12], refs[13]
    reads, writes = [], []
    for k, (src, buf, dst) in enumerate(zip(ins, bufs, outs)):
        n = src.shape[0] // 2
        for i in range(2):
            rows = pl.ds(i * n, n)
            reads.append(pltpu.make_async_copy(src.at[rows], buf.at[rows], sem_in.at[2 * k + i]))
            writes.append(pltpu.make_async_copy(buf.at[rows], dst.at[rows], sem_out.at[2 * k + i]))
    for cp in reads:
        cp.start()
    for rd, wr in zip(reads, writes):
        rd.wait()
        wr.start()
    for wr in writes:
        wr.wait()


def per_device(tokens, cotangent, gate_weight, up_weight, down_weight):
    hbm = pl.BlockSpec(memory_space=pl.ANY)
    rows = 32 * RS
    vm = pltpu.VMEM
    outs = pl.pallas_call(
        kernel,
        out_shape=(
            jax.ShapeDtypeStruct((SLABS * RS, W), F32),
            jax.ShapeDtypeStruct((W, H), F32),
            jax.ShapeDtypeStruct((W, H), F32),
            jax.ShapeDtypeStruct((H, W), F32),
        ),
        in_specs=[hbm] * 5,
        out_specs=[hbm] * 4,
        scratch_shapes=[
            vm((SLABS, 32, 2, RS, W), BF),
            vm((W, 2 * H), BF),
            vm((H, W), BF),
            vm((SLABS, rows, ZW), F32),
            vm((SLABS, 2, 4, CH, ZW), BF),
            vm((SLABS, 2, 4, CH, ZW), BF),
            vm((SLABS, rows, ZW), BF),
            vm((2, 4, CH, W), F32),
            vm((2, CH, W), F32),
            vm((SLABS, 4, CH, W), BF),
            vm((SLABS, 4, CH, W), BF),
            vm((SLABS, 4, CH, W), BF),
            vm((SLABS, 3, CH, W), BF),
            vm((SLABS, 3, RS, W), BF),
            vm((SLABS, 3, RS, W), BF),
            vm((SLABS * RS, W), F32),
            vm((W, 2 * H), F32),
            vm((H, W), F32),
            pltpu.SemaphoreType.DMA((SLABS, NSEM)),
            pltpu.SemaphoreType.DMA((SLABS, NSEM)),
            pltpu.SemaphoreType.DMA((15,)),
        ],
        compiler_params=pltpu.CompilerParams(
            collective_id=0, has_side_effects=True, vmem_limit_bytes=61 * 2**20
        ),
        name="swiglu_backward",
    )(tokens, cotangent, gate_weight, up_weight, down_weight)
    return pl.pallas_call(
        write_out,
        out_shape=[jax.ShapeDtypeStruct(o.shape, o.dtype) for o in outs],
        in_specs=[hbm] * 4,
        out_specs=[hbm] * 4,
        scratch_shapes=[vm(o.shape, o.dtype) for o in outs]
        + [pltpu.SemaphoreType.DMA((8,)), pltpu.SemaphoreType.DMA((8,))],
        name="write_out",
    )(*outs)


def solution(mesh):
    in_specs = (P("col", "row"), P("col", "row"), P("row", "col"), P("row", "col"), P("col", "row"))
    out_specs = (P("col", "row"), P("row", "col"), P("row", "col"), P("col", "row"))
    return jax.shard_map(
        per_device, mesh=mesh, in_specs=in_specs, out_specs=out_specs, check_vma=False
    )
```
